768 devices in a mesh: outer: 16 (over x_hi, y), inner: 48 (over z, x_lo, core).
Axes of the slice: x: 4 (x_hi: 2, x_lo: 2; x = x_hi * 2 + x_lo), y: 8, z: 12, core: 2. Of those that a mesh axis runs over, the one named last changes fastest.
Arguments:
- layer_input: bfloat16 [147456, 8192], P(('outer', 'inner')), may hold values from -6 to 6
- query: bfloat16 [147456, 1024], P(('outer', 'inner')), may hold values from -5 to 5
- keys_values: bfloat16 [147456, 256], P(('outer', 'inner')), may hold values from -5 to 5
- grad_output: bfloat16 [147456, 1024], P(('outer', 'inner')), may hold values from -48 to 48
- logsumexp: float32 [147456, 8], P(('outer', 'inner')), as said below
- delta: float32 [147456, 8], P(('outer', 'inner')), may hold values from -192 to 192
Outputs:
- grad_query: bfloat16 [147456, 1024], P(('outer', 'inner'))
- grad_keys_values: bfloat16 [147456, 256], P(('outer', 'inner'))
- grad_weight: float32 [8192, 256], P('outer')
The draws below stay inside these ranges and needn't reach their ends.
Inputs may be any that keep to these rules, and one draw needn't show every extreme that they name: logsumexp[i, h] exceeds the log-sum-exp of row i's scores over its allowed keys, so that every probs entry is below 1.
All inputs are finite; a program needn't handle non-finite values.
Results may differ from the reference program's by a relative error of at most 0.018.
Values may be sent and summed in bfloat16 or wider, within the bound.
A program may use at most 64 MiB of HBM per device.

```python
import math
import jax
import jax.numpy as jnp
from jax import lax

D = 8192
HD = 128
HQ = 8
WIN = 3
TOK_DEV = 192
SEGMENT = 9216
TOKENS = 147456
N_OUTER = 16
N_INNER = 48


def joint_draw(key):
    base = jax.random.fold_in(key, 4242)
    key_query, key_kv = jax.random.split(base, 2)
    query_vals = jnp.clip(jax.random.normal(key_query, (TOKENS, HQ * HD), jnp.float32), -4.5, 4.5)
    kv_vals = jnp.clip(jax.random.normal(key_kv, (TOKENS, 2 * HD), jnp.float32), -4.5, 4.5)
    return (query_vals.astype(jnp.bfloat16), kv_vals.astype(jnp.bfloat16))


def window_allowed(tok_rows, inner_pos, outer_pos):
    query_pos = lax.broadcasted_iota(jnp.int32, (tok_rows, (WIN + 2) * tok_rows), 0)
    column = lax.broadcasted_iota(jnp.int32, (tok_rows, (WIN + 2) * tok_rows), 1)
    key_slot = column // tok_rows
    key_pos = column % tok_rows
    own_block = (key_slot == 0) & (key_pos <= query_pos)
    near_block = (key_slot >= 1) & (key_slot <= WIN) & (inner_pos >= key_slot)
    memory_block = (key_slot == WIN + 1) & (outer_pos >= 1)
    return own_block | near_block | memory_block


def draw_query(key, part):
    return joint_draw(key)[0]


def draw_keys_values(key, part):
    return joint_draw(key)[1]


def draw_logsumexp(key, part):
    query_vals, kv_vals = joint_draw(key)
    places = SEGMENT // TOK_DEV
    block_count = TOKENS // TOK_DEV
    query_blocks = query_vals.reshape(block_count, TOK_DEV, HQ, HD).astype(jnp.float32)
    kv_blocks = kv_vals.reshape(block_count, TOK_DEV, 2 * HD)[:, :, :HD].astype(jnp.float32)
    gathered = [kv_blocks]
    for offset in range(1, WIN + 1):
        gathered.append(jnp.roll(kv_blocks, offset, axis=0))
    gathered.append(jnp.roll(kv_blocks, places, axis=0))
    key_rows_all = jnp.concatenate(gathered, axis=1)
    block_ids = jnp.arange(block_count, dtype=jnp.int32)

    def one_block(packed):
        query_blk, key_blk, block_id = packed
        scores = jnp.einsum('thd,kd->thk', query_blk, key_blk) * HD ** (-0.5)
        allowed = window_allowed(TOK_DEV, block_id % places, block_id // places)
        scores = jnp.where(allowed[:, None, :], scores, -jnp.inf)
        return jax.nn.logsumexp(scores, axis=-1)
    window_lse = lax.map(one_block, (query_blocks, key_rows_all, block_ids)).reshape(TOKENS, HQ)
    extra = jnp.exp(jax.random.uniform(jax.random.fold_in(key, 77), (TOKENS, HQ), jnp.float32, math.log(0.1), math.log(3.0)))
    return window_lse + jnp.log1p(extra)


def block_levels(rng, shape, shards, smallest, largest):
    loudness = 1.0
    for position, parts in shards:
        draws = jax.random.uniform(jax.random.fold_in(jax.random.fold_in(rng, 6), position), (parts,), jnp.float32, smallest / len(shards), largest / len(shards))
        loudness = loudness * jnp.repeat(jnp.exp(draws), shape[position] // parts).reshape((-1,) + (1,) * (len(shape) - 1 - position))
    return loudness


def gaussian(stream_key, shape, deviation, bound, cuts=(), held_as=jnp.bfloat16):
    result = deviation * jax.random.normal(stream_key, shape, jnp.float32)
    if cuts:
        result = result * block_levels(stream_key, shape, cuts, -0.22, 0.18)
    return jnp.clip(result, -bound, bound).astype(held_as)


def setup_inputs(seed: int = 0) -> dict:
    key_list = jax.random.split(jax.random.key(seed), 7)
    layer_input = gaussian(key_list[0], (TOKENS, D), 1.0, 6.0, ((0, 768),))
    query = draw_query(jax.random.fold_in(key_list[6], 71), 0)
    keys_values = draw_keys_values(jax.random.fold_in(key_list[6], 71), 0)
    grad_output = gaussian(key_list[3], (TOKENS, HQ * HD), 8.0, 48.0, ((0, 768),))
    logsumexp = draw_logsumexp(jax.random.fold_in(key_list[6], 71), 0)
    delta = gaussian(key_list[5], (TOKENS, HQ), 32.0, 192.0, ((0, 768),), jnp.float32)
    return dict(layer_input=layer_input, query=query, keys_values=keys_values, grad_output=grad_output, logsumexp=logsumexp, delta=delta)


def make_allowed(tok_rows, inner_pos, outer_pos):
    query_pos = lax.broadcasted_iota(jnp.int32, (tok_rows, (WIN + 2) * tok_rows), 0)
    column = lax.broadcasted_iota(jnp.int32, (tok_rows, (WIN + 2) * tok_rows), 1)
    key_slot = column // tok_rows
    key_pos = column % tok_rows
    own_block = (key_slot == 0) & (key_pos <= query_pos)
    near_block = (key_slot >= 1) & (key_slot <= WIN) & (inner_pos >= key_slot)
    memory_block = (key_slot == WIN + 1) & (outer_pos >= 1)
    return own_block | near_block | memory_block


def local_grads(query_blk, key_rows_all, grad_blk, lse_blk, delta_blk, inner_pos, outer_pos):
    tok_rows = query_blk.shape[0]
    scaling = HD ** -0.5
    query_heads = query_blk.reshape(tok_rows, HQ, HD).astype(jnp.float32)
    grad_heads = grad_blk.reshape(tok_rows, HQ, HD).astype(jnp.float32)
    keys_float = key_rows_all[:, :HD].astype(jnp.float32)
    values_float = key_rows_all[:, HD:].astype(jnp.float32)
    scores = jnp.einsum('thd,kd->htk', query_heads, keys_float) * scaling
    allowed = make_allowed(tok_rows, inner_pos, outer_pos)
    scores = jnp.where(allowed[None], scores, -jnp.inf)
    probs = jnp.exp(scores - jnp.transpose(lse_blk)[:, :, None])
    probs_half = probs.astype(jnp.bfloat16)
    grad_probs = jnp.einsum('thd,kd->htk', grad_heads, values_float)
    grad_scores = (probs * (grad_probs - jnp.transpose(delta_blk)[:, :, None]) * scaling).astype(jnp.bfloat16)
    grad_float = grad_scores.astype(jnp.float32)
    grad_query = jnp.einsum('htk,kd->thd', grad_float, keys_float)
    grad_query = grad_query.reshape(tok_rows, HQ * HD).astype(jnp.bfloat16)
    grad_keys = jnp.einsum('htk,thd->kd', grad_float, query_heads)
    grad_values = jnp.einsum('htk,thd->kd', probs_half.astype(jnp.float32), grad_heads)
    return grad_query, jnp.concatenate([grad_keys, grad_values], axis=-1)


def reference(layer_input, query, keys_values, grad_output, logsumexp, delta):
    block_count = N_OUTER * N_INNER
    query_blocks = query.reshape(block_count, TOK_DEV, HQ * HD)
    grad_blocks = grad_output.reshape(block_count, TOK_DEV, HQ * HD)
    lse_blocks = logsumexp.reshape(block_count, TOK_DEV, HQ)
    delta_blocks = delta.reshape(block_count, TOK_DEV, HQ)
    kv_blocks = keys_values.reshape(block_count, TOK_DEV, 2 * HD)
    gathered = [kv_blocks]
    for offset in range(1, WIN + 1):
        gathered.append(jnp.roll(kv_blocks, offset, axis=0))
    gathered.append(jnp.roll(kv_blocks, N_INNER, axis=0))
    key_rows_all = jnp.concatenate(gathered, axis=1)
    block_ids = jnp.arange(block_count, dtype=jnp.int32)

    def one_block(packed):
        query_blk, key_blk, grad_blk, lse_blk, delta_blk, block_id = packed
        return local_grads(query_blk, key_blk, grad_blk, lse_blk, delta_blk, block_id % N_INNER, block_id // N_INNER)

    grad_query, grad_terms = lax.map(one_block, (query_blocks, key_rows_all, grad_blocks, lse_blocks, delta_blocks, block_ids))
    pieces = grad_terms.reshape(block_count, WIN + 2, TOK_DEV, 2 * HD)
    summed = pieces[:, 0]
    for offset in range(1, WIN + 1):
        summed = summed + jnp.roll(pieces[:, offset], -offset, axis=0)
    summed = summed + jnp.roll(pieces[:, WIN + 1], -N_INNER, axis=0)
    grad_kv = summed.astype(jnp.bfloat16)
    input_blocks = layer_input.reshape(block_count, TOK_DEV, D)

    def add_block(running, packed):
        input_blk, grad_blk = packed
        partial_sum = jnp.dot(input_blk.T, grad_blk, preferred_element_type=jnp.float32).astype(jnp.bfloat16)
        partial_sum = lax.optimization_barrier(partial_sum)
        return running + partial_sum.astype(jnp.float32), None

    grad_weight, _ = lax.scan(add_block, jnp.zeros((D, 2 * HD), jnp.float32), (input_blocks, grad_kv))
    return (grad_query.reshape(TOKENS, HQ * HD), grad_kv.reshape(TOKENS, 2 * HD), grad_weight)
```

```python
import functools

import jax
import jax.numpy as jnp
from jax import lax
from jax.experimental import pallas as pl
from jax.experimental.pallas import tpu as pltpu
from jax.sharding import Mesh
from jax.sharding import PartitionSpec as P

HD = 128
HQ = 8
WIN = 3
AXES = ("x_hi", "y", "z", "x_lo", "core")
MESH = pl.DeviceIdType.MESH
BF16 = jnp.bfloat16
F32 = jnp.float32
NT = (((1,), (1,)), ((), ()))


def dot(a, b):
    return jnp.dot(a, b, preferred_element_type=F32)


def dot_nt(a, b):
    return lax.dot_general(a, b, NT, preferred_element_type=F32)


def kernel(
    ny, nz, tok, chunk,
    x_hbm, q_hbm, kv_hbm, do_hbm, lse_hbm, delta_hbm,
    dq_out, gkv_out, gw_out,
    qs, dos, lse_in, delta_in, rows, kvb, ds_all, gsend, grecv, xa, xb, g6, gt,
    keep, xs, xr, ys, yr, zsrc, zr, za, fin,
    load_sem, xl_sem, kv_send, kv_recv, gr_send, gr_recv, xsnd, xrcv, g_send, g_recv,
    xs_send, xs_recv, y_send, y_recv, zr_send, zr_recv, za_send, za_recv, f_send, f_recv,
):
    h = lax.axis_index("x_hi")
    y = lax.axis_index("y")
    z = lax.axis_index("z")
    l = lax.axis_index("x_lo")
    c = lax.axis_index("core")
    n_inner = nz * 4
    inner = z * 4 + l * 2 + c
    n_outer = 2 * ny
    outer = h * ny + y
    scaling = HD ** (-0.5)

    def inner_dev(step):
        j = lax.rem(inner + step + n_inner, n_inner)
        return {"z": j // 4, "x_lo": lax.rem(j // 2, 2), "core": lax.rem(j, 2)}

    def outer_dev(step):
        j = lax.rem(outer + step + n_outer, n_outer)
        return {"x_hi": j // ny, "y": lax.rem(j, ny)}

    core_dev = {"core": 1 - c}
    p1_same = {"x_lo": 1 - l}
    p1_other = {"x_lo": 1 - l, "core": 1 - c}
    p2_same = {"x_hi": 1 - h, "x_lo": 1 - l}
    p2_other = {"x_hi": 1 - h, "x_lo": 1 - l, "core": 1 - c}

    def y_dev(d):
        return {"y": lax.rem(y + d, ny)}

    def z_dev(d):
        return {"z": lax.rem(z + d, nz)}

    def remote(src, dst, send, recv, device):
        return pltpu.make_async_remote_copy(
            src_ref=src, dst_ref=dst, send_sem=send, recv_sem=recv, device_id=device, device_id_type=MESH
        )

    loads = []
    for k in range(HQ):
        part, cols = pl.ds(k * tok, tok), pl.ds(k * HD, HD)
        loads.append(pltpu.make_async_copy(q_hbm.at[:, cols], qs.at[part, :], load_sem.at[k]))
        loads.append(pltpu.make_async_copy(do_hbm.at[:, cols], dos.at[part, :], load_sem.at[HQ + k]))
    loads.append(pltpu.make_async_copy(lse_hbm, lse_in, load_sem.at[2 * HQ]))
    loads.append(pltpu.make_async_copy(delta_hbm, delta_in, load_sem.at[2 * HQ + 1]))
    loads.append(pltpu.make_async_copy(kv_hbm, kvb.at[0], load_sem.at[2 * HQ + 2]))
    for copy in loads:
        copy.start()

    greeted = [inner_dev(s) for s in (1, 2, 3, -1, -2, -3)] + [outer_dev(1), outer_dev(-1)]
    greeted += [core_dev, p1_same, p1_other, p2_same, p2_other]
    greeted += [y_dev(d) for d in range(1, ny)] + [z_dev(d) for d in range(1, nz)]
    barrier = pltpu.get_barrier_semaphore()
    for device in greeted:
        pl.semaphore_signal(barrier, inc=1, device_id=device, device_id_type=MESH)
    pl.semaphore_wait(barrier, len(greeted))

    kv_copies = []
    for w in range(1, WIN + 2):
        device = inner_dev(w) if w <= WIN else outer_dev(1)
        kv_copies.append(remote(kv_hbm, kvb.at[w], kv_send.at[w - 1], kv_recv.at[w - 1], device))
        kv_copies[-1].start()

    half = ny // 2
    shard = 512

    def columns(hh, ll, cc, d):
        yy = lax.rem(y + d, ny)
        return pl.ds(pl.multiple_of((hh * ny + yy) * shard + (cc * 2 + ll) * 128, 128), 128)

    def send_columns(k, carry):
        d_a, d_b = half + k, half - 1 - k

        def slot(s):
            return pl.ds(pl.multiple_of(k * 256 + s * 128, 128), 128)

        for s in range(2):
            def from_a(hh, ll, cc):
                return x_hbm.at[:, columns(1 - hh if s else hh, 1 - ll if s else ll, cc, d_a)]

            def from_b(hh, ll, cc):
                return x_hbm.at[:, columns(hh, 1 - ll if s else ll, cc, d_b)]

            pltpu.make_async_copy(from_a(h, l, c), xa.at[pl.ds(2 * tok, tok), slot(s)], xl_sem.at[0]).start()
            pltpu.make_async_copy(from_b(h, l, c), xb.at[pl.ds(0, tok), slot(s)], xl_sem.at[1]).start()
            remote(from_a(h, 1 - l, c), xa.at[pl.ds(0, tok), slot(s)], xsnd.at[0], xrcv.at[0], p1_same).start()
            remote(
                from_b(1 - h, 1 - l, c), xb.at[pl.ds(2 * tok, tok), slot(s)], xsnd.at[1], xrcv.at[1], p2_same
            ).start()
            remote(
                from_a(h, 1 - l, 1 - c), xa.at[pl.ds(tok, tok), slot(s)], xsnd.at[2], xrcv.at[2], p1_other
            ).start()
            remote(
                from_b(1 - h, 1 - l, 1 - c), xb.at[pl.ds(3 * tok, tok), slot(s)], xsnd.at[3], xrcv.at[3], p2_other
            ).start()
            remote(
                from_a(h, l, 1 - c), xa.at[pl.ds(3 * tok, tok), slot(s)], xsnd.at[4], xrcv.at[4], core_dev
            ).start()
            remote(from_b(h, l, 1 - c), xb.at[pl.ds(tok, tok), slot(s)], xsnd.at[5], xrcv.at[5], core_dev).start()
        return carry

    lax.fori_loop(0, half, send_columns, 0)
    x_places = [
        (xa, 0, p1_same), (xb, 2, p2_same), (xa, 1, p1_other), (xb, 3, p2_other), (xa, 3, core_dev), (xb, 1, core_dev)
    ]
    x_copies = []
    for k, (buffer, place, device) in enumerate(x_places):
        whole = buffer.at[pl.ds(place * tok, tok), :]
        x_copies.append(remote(whole, whole, xsnd.at[k], xrcv.at[k], device))

    for copy in loads:
        copy.wait()
    for k in range(HQ):
        rows[0:1, k * tok : (k + 1) * tok] = lse_in[k : k + 1, :]
        rows[8:9, k * tok : (k + 1) * tok] = delta_in[k : k + 1, :]

    wide = 2 * tok
    key_pos = lax.broadcasted_iota(jnp.int32, (tok, wide), 0)
    lane = lax.broadcasted_iota(jnp.int32, (tok, wide), 1)
    query_pos = jnp.where(lane >= tok, lane - tok, lane)
    causal = key_pos <= query_pos

    def attend(w):
        key = kvb[w, :, :HD]
        value = kvb[w, :, HD:]
        if w == 0:
            penalty = None
        elif w <= WIN:
            penalty = jnp.where(inner >= w, 0.0, 1e30).astype(F32)
        else:
            penalty = jnp.where(outer >= 1, 0.0, 1e30).astype(F32)
        grad_key = jnp.zeros((tok, HD), F32)
        grad_value = jnp.zeros((tok, HD), F32)
        for k in range(HQ // 2):
            part = slice(k * wide, (k + 1) * wide)
            query, cotangent = qs[part, :], dos[part, :]
            lse, delta = rows[0:1, part], rows[8:9, part]
            if penalty is not None:
                lse = lse + penalty
            scores = dot_nt(key, query) * scaling - lse
            if penalty is None:
                scores = jnp.where(causal, scores, -1e30)
            probs = jnp.exp(scores)
            grad_probs = dot_nt(value, cotangent)
            grad_scores = (probs * (grad_probs - delta) * scaling).astype(BF16)
            ds_all[w * tok : (w + 1) * tok, part] = grad_scores
            grad_key = grad_key + dot(grad_scores, query)
            grad_value = grad_value + dot(probs.astype(BF16), cotangent)
        return grad_key, grad_value

    own_key, own_value = attend(0)
    grad_copies = {}
    for w in (3, 4, 2, 1):
        kv_copies[w - 1].wait_recv()
        grad_key, grad_value = attend(w)
        gsend[w - 1, :, :HD] = grad_key.astype(BF16)
        gsend[w - 1, :, HD:] = grad_value.astype(BF16)
        device = inner_dev(-w) if w <= WIN else outer_dev(-1)
        grad_copies[w] = remote(
            gsend.at[w - 1], grecv.at[w - 1], gr_send.at[w - 1], gr_recv.at[w - 1], device
        )
        grad_copies[w].start()

    keys_all = jnp.concatenate([kvb[w, :, :HD] for w in range(WIN + 2)], axis=0)
    keys_t = keys_all.T
    for k in range(HQ // 2):
        part = slice(k * wide, (k + 1) * wide)
        turned = dot(keys_t, ds_all[:, part]).T.astype(BF16)
        dq_out[:, 2 * k * HD : (2 * k + 1) * HD] = turned[:tok]
        dq_out[:, (2 * k + 1) * HD : (2 * k + 2) * HD] = turned[tok:]

    for w in (3, 4, 2, 1):
        grad_copies[w].wait_recv()
        own_key = own_key + grecv[w - 1, :, :HD].astype(F32)
        own_value = own_value + grecv[w - 1, :, HD:].astype(F32)
    grad_kv = jnp.concatenate([own_key, own_value], axis=1).astype(BF16)
    own_rows = pl.ds(2 * tok, tok)
    g6[own_rows, :] = grad_kv
    gkv_out[...] = grad_kv

    g_copies = []
    for k, (place, device) in enumerate(
        ((3, core_dev), (0, p1_same), (4, p2_same), (1, p1_other), (5, p2_other))
    ):
        g_copies.append(
            remote(g6.at[own_rows, :], g6.at[pl.ds(place * tok, tok), :], g_send.at[k], g_recv.at[k], device)
        )
        g_copies[-1].start()

    def turn(pair):
        gt[:, pair * wide : (pair + 1) * wide] = g6[pair * wide : (pair + 1) * wide, :].T

    own_a = xa.at[pl.ds(2 * tok, tok), :]
    own_b = xb.at[pl.ds(0, tok), :]
    pltpu.make_async_copy(own_a, own_a, xl_sem.at[0]).wait()
    pltpu.make_async_copy(own_b, own_b, xl_sem.at[1]).wait()
    g_copies[0].wait_recv()
    turn(1)
    for k in (1, 3):
        g_copies[k].wait_recv()
    turn(0)
    for k in (2, 4):
        g_copies[k].wait_recv()
    turn(2)
    for copy in x_copies:
        copy.wait_recv()

    order = []
    for k in range(half):
        order += [half + k, half - 1 - k]
    x_sums = {}
    for d in order:
        if d >= half:
            k = d - half
            product = dot(gt[:, : 4 * tok], xa[:, k * 256 : (k + 1) * 256])
        else:
            k = half - 1 - d
            product = dot(gt[:, 2 * tok :], xb[:, k * 256 : (k + 1) * 256])
        keep[d] = product[:, :128]
        xs[d] = product[:, 128:].astype(BF16)
        x_sums[d] = remote(
            xs.at[d], xr.at[d], xs_send.at[d], xs_recv.at[d], p2_same if d >= half else p1_same
        )
        x_sums[d].start()

    y_sums = {}
    for d in order:
        x_sums[d].wait_recv()
        total = keep[d] + xr[d].astype(F32)
        if d == 0:
            own_total = total
        else:
            ys[d] = total.astype(BF16)
            y_sums[d] = remote(ys.at[d], yr.at[d], y_send.at[d], y_recv.at[d], y_dev(d))
            y_sums[d].start()
    for d in order:
        if d != 0:
            y_sums[d].wait_recv()
            own_total = own_total + yr[d].astype(F32)

    zsrc[0:256, :] = own_total
    if chunk * nz > 256:
        zsrc[256:, :] = jnp.zeros((chunk * nz - 256, 128), F32)
    z_order = sorted(range(1, nz), key=lambda d: -min(d, nz - d))
    z_sums = {}
    for d in z_order:
        there = lax.rem(z + d, nz)
        z_sums[d] = remote(
            zsrc.at[pl.ds(pl.multiple_of(there * chunk, 8), chunk), :], zr.at[d], zr_send.at[d], zr_recv.at[d], z_dev(d)
        )
        z_sums[d].start()
    here = pl.ds(pl.multiple_of(z * chunk, 8), chunk)
    piece = zsrc[here, :]
    for d in reversed(z_order):
        z_sums[d].wait_recv()
        piece = piece + zr[d]
    za[here, :] = piece
    z_all = {}
    for d in z_order:
        z_all[d] = remote(za.at[here, :], za.at[here, :], za_send.at[d], za_recv.at[d], z_dev(d))
        z_all[d].start()
    for d in reversed(z_order):
        z_all[d].wait_recv()

    quarter = c * 2 + l
    place = pl.ds(pl.multiple_of(quarter * 128, 128), 128)
    fin[place, :] = za[0:256, :].T.astype(BF16)
    ends = []
    for k, device in enumerate((p1_same, p1_other, core_dev)):
        ends.append(remote(fin.at[place, :], fin.at[place, :], f_send.at[k], f_recv.at[k], device))
        ends[-1].start()
    for copy in ends:
        copy.wait_recv()
    gw_out[...] = fin[...]

    for copy in kv_copies + list(grad_copies.values()) + x_copies + g_copies + list(x_sums.values()):
        copy.wait_send()
    for copy in list(y_sums.values()) + list(z_sums.values()) + list(z_all.values()) + ends:
        copy.wait_send()


def local(ny, nz, layer_input, query, keys_values, grad_output, logsumexp, delta):
    tok = query.shape[0]
    heads = HQ * tok
    chunk = -(-32 // nz) * 8
    dma = pltpu.SemaphoreType.DMA
    half = ny // 2
    any_spec = pl.BlockSpec(memory_space=pl.ANY)
    vmem_spec = pl.BlockSpec(memory_space=pltpu.VMEM)
    grad_query, grad_kv, grad_weight = pl.pallas_call(
        functools.partial(kernel, ny, nz, tok, chunk),
        out_shape=(
            jax.ShapeDtypeStruct((tok, HQ * HD), BF16),
            jax.ShapeDtypeStruct((tok, 2 * HD), BF16),
            jax.ShapeDtypeStruct((512, 2 * HD), BF16),
        ),
        in_specs=[any_spec] * 6,
        out_specs=(vmem_spec, vmem_spec, vmem_spec),
        scratch_shapes=[
            pltpu.VMEM((heads, HD), BF16),
            pltpu.VMEM((heads, HD), BF16),
            pltpu.VMEM((HQ, tok), F32),
            pltpu.VMEM((HQ, tok), F32),
            pltpu.VMEM((16, heads), F32),
            pltpu.VMEM((WIN + 2, tok, 2 * HD), BF16),
            pltpu.VMEM(((WIN + 2) * tok, heads), BF16),
            pltpu.VMEM((WIN + 1, tok, 2 * HD), BF16),
            pltpu.VMEM((WIN + 1, tok, 2 * HD), BF16),
            pltpu.VMEM((4 * tok, half * 256), BF16),
            pltpu.VMEM((4 * tok, half * 256), BF16),
            pltpu.VMEM((6 * tok, 2 * HD), BF16),
            pltpu.VMEM((2 * HD, 6 * tok), BF16),
            pltpu.VMEM((ny, 256, 128), F32),
            pltpu.VMEM((ny, 256, 128), BF16),
            pltpu.VMEM((ny, 256, 128), BF16),
            pltpu.VMEM((ny, 256, 128), BF16),
            pltpu.VMEM((ny, 256, 128), BF16),
            pltpu.VMEM((chunk * nz, 128), F32),
            pltpu.VMEM((nz, chunk, 128), F32),
            pltpu.VMEM((chunk * nz, 128), F32),
            pltpu.VMEM((512, 2 * HD), BF16),
            dma((2 * HQ + 3,)),
            dma((2,)),
            dma((WIN + 1,)),
            dma((WIN + 1,)),
            dma((WIN + 1,)),
            dma((WIN + 1,)),
            dma((6,)),
            dma((6,)),
            dma((5,)),
            dma((5,)),
            dma((ny,)),
            dma((ny,)),
            dma((ny,)),
            dma((ny,)),
            dma((nz,)),
            dma((nz,)),
            dma((nz,)),
            dma((nz,)),
            dma((3,)),
            dma((3,)),
        ],
        compiler_params=pltpu.CompilerParams(
            collective_id=0, has_side_effects=True, vmem_limit_bytes=56 * 1024 * 1024
        ),
    )(layer_input, query, keys_values, grad_output, logsumexp.T, delta.T)
    return grad_query, grad_kv, grad_weight.astype(F32)


def solution(mesh):
    ny = mesh.shape["outer"] // 2
    nz = mesh.shape["inner"] // 4
    finer = Mesh(mesh.devices.reshape(2, ny, nz, 2, 2), AXES)
    tokens = P(AXES, None)
    return jax.shard_map(
        functools.partial(local, ny, nz),
        mesh=finer,
        in_specs=(tokens,) * 6,
        out_specs=(tokens, tokens, P(("x_hi", "y"), None)),
        check_vma=False,
    )
```

```python
import functools

import jax
import jax.numpy as jnp
from jax import lax
from jax.experimental import pallas as pl
from jax.experimental.pallas import tpu as pltpu
from jax.sharding import Mesh
from jax.sharding import PartitionSpec as P

HD = 128
HQ = 8
WIN = 3
AXES = ("x_hi", "y", "z", "x_lo", "core")
MESH = pl.DeviceIdType.MESH
BF16 = jnp.bfloat16
F32 = jnp.float32
NT = (((1,), (1,)), ((), ()))
LOG2E = 1.4426950408889634


def dot(a, b):
    return jnp.dot(a, b, preferred_element_type=F32)


def dot_nt(a, b):
    return lax.dot_general(a, b, NT, preferred_element_type=F32)


def kernel(
    ny, nz, tok, lists, owners,
    x_hbm, q_hbm, kv_hbm, do_hbm, lse_hbm, delta_hbm,
    dq_out, gkv_out, gw_out,
    qs, dos, lse_in, delta_in, rows, kvb, ds_all, gsend, grecv, x_own, x_pair, gs, gt,
    keep, xs, xr, ys, yr, zsrc, zr, fin,
    load_sem, x_local, kv_send, kv_recv, gr_send, gr_recv, xsnd, xrcv, g_send, g_recv,
    xs_send, xs_recv, y_send, y_recv, zr_send, zr_recv, za_send, za_recv, f_send, f_recv,
):
    h = lax.axis_index("x_hi")
    y = lax.axis_index("y")
    z = lax.axis_index("z")
    l = lax.axis_index("x_lo")
    c = lax.axis_index("core")
    n_inner = nz * 4
    inner = z * 4 + l * 2 + c
    n_outer = 2 * ny
    outer = h * ny + y
    scaling = HD ** (-0.5)

    def inner_dev(step):
        j = lax.rem(inner + step + n_inner, n_inner)
        return {"z": j // 4, "x_lo": lax.rem(j // 2, 2), "core": lax.rem(j, 2)}

    def outer_dev(step):
        j = lax.rem(outer + step + n_outer, n_outer)
        return {"x_hi": j // ny, "y": lax.rem(j, ny)}

    z_m = lax.rem(z + 1 - 2 * l + nz, nz)
    z_n = lax.rem(z - 1 + 2 * l + nz, nz)
    core_dev = {"core": 1 - c}
    p1_same = {"x_lo": 1 - l}
    p1_other = {"x_lo": 1 - l, "core": 1 - c}
    p2_same = {"x_hi": 1 - h, "x_lo": 1 - l}
    p2_other = {"x_hi": 1 - h, "x_lo": 1 - l, "core": 1 - c}
    zm_same, zm_other = {"z": z_m}, {"z": z_m, "core": 1 - c}
    zn_same, zn_other = {"z": z_n}, {"z": z_n, "core": 1 - c}

    def y_dev(d):
        return {"y": lax.rem(y + d, ny)}

    def z_dev(d):
        return {"z": lax.rem(z + d, nz)}

    def remote(src, dst, send, recv, device):
        return pltpu.make_async_remote_copy(
            src_ref=src, dst_ref=dst, send_sem=send, recv_sem=recv, device_id=device, device_id_type=MESH
        )

    z_order = sorted(range(1, nz), key=lambda d: -min(d, nz - d))
    y_order = sorted(range(1, ny), key=lambda d: -min(d, ny - d))

    loads = []
    for k in range(HQ):
        part, cols = pl.ds(k * tok, tok), pl.ds(k * HD, HD)
        pltpu.make_async_copy(q_hbm.at[:, cols], qs.at[part, :], load_sem.at[0]).start()
        pltpu.make_async_copy(do_hbm.at[:, cols], dos.at[part, :], load_sem.at[1]).start()
    loads.append(pltpu.make_async_copy(lse_hbm, lse_in, load_sem.at[2]))
    loads.append(pltpu.make_async_copy(delta_hbm, delta_in, load_sem.at[3]))
    loads.append(pltpu.make_async_copy(kv_hbm, kvb.at[0], load_sem.at[4]))
    for copy in loads:
        copy.start()
    loads.append(pltpu.make_async_copy(qs, qs, load_sem.at[0]))
    loads.append(pltpu.make_async_copy(dos, dos, load_sem.at[1]))

    with jax.named_scope("greet"):
        greeted = [z_dev(d) for d in z_order] + [y_dev(d) for d in y_order] + [outer_dev(1), outer_dev(-1)]
        greeted += [inner_dev(6 * c - 3), inner_dev(2), inner_dev(-2)]
        greeted += [p1_other, p2_other, zm_other, zn_other, p1_same, p2_same, core_dev]
        barrier = pltpu.get_barrier_semaphore()
        for device in greeted:
            pl.semaphore_signal(barrier, inc=1, device_id=device, device_id_type=MESH)
        pl.semaphore_wait(barrier, len(greeted))

    before = (0, 2, 1 + 2 * c, 3 - 2 * c)
    kv_copies = {}
    for slot, device in ((1, inner_dev(2)), (3, inner_dev(1 + 2 * c)), (4, outer_dev(1))):
        kv_copies[slot] = remote(kv_hbm, kvb.at[slot], kv_send.at[slot - 1], kv_recv.at[slot - 1], device)
        kv_copies[slot].start()

    far = 1 - lax.rem(l + z, 2)
    steps_a, steps_b, steps_c, steps_e = lists
    size = len(steps_a)
    distances = [
        list(steps_a),
        list(steps_b),
        [e + far * (s - e) for s, e in zip(steps_c, steps_e)],
        [s + far * (e - s) for s, e in zip(steps_c, steps_e)],
    ]
    def places(which, hh, ll):
        return (
            ((hh, ll), (1 - hh, 1 - ll)),
            ((hh, ll), (hh, 1 - ll)),
            ((hh, ll), (1 - hh, ll)),
            ((hh, 1 - ll), (1 - hh, 1 - ll)),
        )[which]

    shard = 512
    pairs = (
        (0, 0, (h, 1 - l), p1_same, p1_other),
        (1, 1, (1 - h, 1 - l), p2_same, p2_other),
        (2, 3, (h, l), zm_same, zm_other),
        (3, 2, (h, l), zn_same, zn_other),
    )
    with jax.named_scope("issue_columns"):
        for k in range(size):
            for s in range(2):
                slot = pl.ds(k * 256 + s * 128, 128)
                for mine, theirs, (hh, ll), same, other in pairs:
                    shards = lax.rem(y + distances[mine][k], ny) * shard

                    def columns(place, cc):
                        start = place[0] * (ny * shard) + shards + (cc * 2 + place[1]) * 128
                        return x_hbm.at[:, pl.ds(pl.multiple_of(start, 128), 128)]

                    there = places(theirs, hh, ll)[s]
                    here = places(mine, h, l)[s]
                    remote(
                        columns(there, c), x_pair.at[theirs, pl.ds(0, tok), slot],
                        xsnd.at[0], xrcv.at[theirs], same,
                    ).start()
                    remote(
                        columns(there, 1 - c), x_pair.at[theirs, pl.ds(tok, tok), slot],
                        xsnd.at[1], xrcv.at[theirs], other,
                    ).start()
                    remote(
                        columns(here, 1 - c), x_own.at[mine, pl.ds(tok, tok), slot],
                        xsnd.at[2], xrcv.at[4], core_dev,
                    ).start()
                    pltpu.make_async_copy(
                        columns(here, c), x_own.at[mine, pl.ds(0, tok), slot], x_local.at[0]
                    ).start()
    from_own = x_own.at[:, pl.ds(0, tok), :]
    from_core = x_own.at[:, pl.ds(tok, tok), :]
    from_same = x_pair.at[:, pl.ds(0, tok), :]
    from_other = x_pair.at[:, pl.ds(tok, tok), :]

    with jax.named_scope("load_wait"):
        for copy in loads:
            copy.wait()
    for k in range(HQ):
        rows[0:1, k * tok : (k + 1) * tok] = lse_in[k : k + 1, :] * LOG2E
        rows[8:9, k * tok : (k + 1) * tok] = delta_in[k : k + 1, :]

    wide = 2 * tok
    heads = HQ // 2
    key_pos = lax.broadcasted_iota(jnp.int32, (tok, heads * tok), 0)
    lane = lax.broadcasted_iota(jnp.int32, (tok, heads * tok), 1)
    causal = key_pos <= lax.rem(lane, tok)

    def attend(w):
        key = kvb[w, :, :HD]
        value = kvb[w, :, HD:]
        if w == 0:
            penalty = None
        elif w <= WIN:
            penalty = jnp.where(inner >= before[w], 0.0, 1e30).astype(F32)
        else:
            penalty = jnp.where(outer >= 1, 0.0, 1e30).astype(F32)
        grad_key = jnp.zeros((tok, HD), F32)
        grad_value = jnp.zeros((tok, HD), F32)
        for k in range(HQ // heads):
            part = slice(k * heads * tok, (k + 1) * heads * tok)
            query, cotangent = qs[part, :], dos[part, :]
            lse, delta = rows[0:1, part], rows[8:9, part]
            if penalty is not None:
                lse = lse + penalty
            scores = dot_nt(key, query) * (scaling * LOG2E) - lse
            if penalty is None:
                scores = jnp.where(causal, scores, -1e30)
            probs = jnp.exp2(scores)
            grad_probs = dot_nt(value, cotangent)
            grad_scores = (probs * (grad_probs - delta) * scaling).astype(BF16)
            ds_all[w * tok : (w + 1) * tok, part] = grad_scores
            grad_key = grad_key + dot(grad_scores, query)
            grad_value = grad_value + dot(probs.astype(BF16), cotangent)
        return grad_key, grad_value

    with jax.named_scope("own_block"):
        own_key, own_value = attend(0)
    with jax.named_scope("kv_wait"):
        kv_copies[1].wait_recv()
        kv_copies[2] = remote(kvb.at[1], kvb.at[2], kv_send.at[1], kv_recv.at[1], core_dev)
        kv_copies[2].start()
    grad_copies = {}
    for w, device in ((3, inner_dev(2 * c - 3)), (4, outer_dev(-1)), (2, core_dev), (1, inner_dev(-2))):
        if w != 1:
            with jax.named_scope("kv_wait"):
                kv_copies[w].wait_recv()
        with jax.named_scope("attend"):
            grad_key, grad_value = attend(w)
        if w == 1:
            with jax.named_scope("merge_wait"):
                grad_copies[2].wait_recv()
            grad_key = grad_key + grecv[1, :, :HD].astype(F32)
            grad_value = grad_value + grecv[1, :, HD:].astype(F32)
        gsend[w - 1, :, :HD] = grad_key.astype(BF16)
        gsend[w - 1, :, HD:] = grad_value.astype(BF16)
        grad_copies[w] = remote(
            gsend.at[w - 1], grecv.at[w - 1], gr_send.at[w - 1], gr_recv.at[w - 1], device
        )
        grad_copies[w].start()

    with jax.named_scope("grad_query"):
        keys_t = jnp.concatenate([kvb[w, :, :HD] for w in range(WIN + 2)], axis=0).T
        for k in range(HQ // 2):
            part = slice(k * wide, (k + 1) * wide)
            turned = dot(keys_t, ds_all[:, part]).T.astype(BF16)
            dq_out[:, 2 * k * HD : (2 * k + 1) * HD] = turned[:tok]
            dq_out[:, (2 * k + 1) * HD : (2 * k + 2) * HD] = turned[tok:]

    with jax.named_scope("grads_wait"):
        for w in (3, 4, 1):
            grad_copies[w].wait_recv()
            own_key = own_key + grecv[w - 1, :, :HD].astype(F32)
            own_value = own_value + grecv[w - 1, :, HD:].astype(F32)
    grad_kv = jnp.concatenate([own_key, own_value], axis=1).astype(BF16)
    gs[0:tok, :] = grad_kv

    g_copies = {}
    for place, device in ((2, p1_same), (4, p2_same), (8, zm_same), (6, zn_same), (1, core_dev)):
        g_copies[place] = remote(
            gs.at[pl.ds(0, tok), :], gs.at[pl.ds(place * tok, tok), :], g_send.at[0], g_recv.at[place], device
        )
        g_copies[place].start()
    gkv_out[...] = grad_kv

    def turn(pair):
        gt[:, pair * wide : (pair + 1) * wide] = gs[pair * wide : (pair + 1) * wide, :].T

    x_sums = {}

    def push(slot, value, device):
        xs[slot] = value.astype(BF16)
        x_sums[slot] = remote(xs.at[slot], xr.at[slot], xs_send.at[0], xs_recv.at[slot], device)
        x_sums[slot].start()

    with jax.named_scope("core_wait"):
        pltpu.make_async_copy(from_own, from_own, x_local.at[0]).wait()
        remote(from_core, from_core, xsnd.at[2], xrcv.at[4], core_dev).wait_recv()
        g_copies[1].wait_recv()
        turn(0)
    with jax.named_scope("pass_on"):
        for place in (6, 2, 4, 8):
            g_copies[place].wait_recv()
            g_copies[place + 1] = remote(
                gs.at[pl.ds(place * tok, tok), :], gs.at[pl.ds((place + 1) * tok, tok), :],
                g_send.at[0], g_recv.at[place + 1], core_dev,
            )
            g_copies[place + 1].start()

    for mine in (2, 0, 1, 3):
        with jax.named_scope("pair_wait"):
            place = {0: 2, 1: 4, 2: 6, 3: 8}[mine]
            g_copies[place + 1].wait_recv()
            turn(place // 2)
            remote(x_pair.at[mine], x_pair.at[mine], xsnd.at[0], xrcv.at[mine], pairs[mine][3]).wait_recv()
        with jax.named_scope("multiply"):
            for k in range(size):
                cols = slice(k * 256, (k + 1) * 256)
                product = dot(gt[:, :wide], x_own[mine, :, cols])
                product = product + dot(gt[:, place * tok : (place + 2) * tok], x_pair[mine, :, cols])
                first, second = product[:, :128], product[:, 128:]
                if mine == 3:
                    through = 2 * size + k
                    x_sums[through].wait_recv()
                    if k % 2 == 0:
                        second = second + xr[through].astype(F32)
                    else:
                        first = first + xr[through].astype(F32)
                    push(3 * size + k, first, p1_same)
                    push(4 * size + k, second, p2_same)
                else:
                    keep[mine * size + k] = first
                    push(mine * size + k, second, (p2_same, p1_same, p2_same if k % 2 else p1_same)[mine])

    y_sums = {}
    own_total = None
    with jax.named_scope("x_sum"):
        for mine in (0, 1, 2):
            for k in range(size):
                slot = mine * size + k
                total = keep[slot]
                for source in (3 * size + k, 4 * size + k) if mine == 2 else (slot,):
                    x_sums[source].wait_recv()
                    total = total + xr[source].astype(F32)
                distance = distances[mine][k]
                if mine < 2 and distance == 0:
                    own_total = total
                else:
                    ys[slot] = total.astype(BF16)
                    y_sums[slot] = remote(
                        ys.at[slot], yr.at[slot], y_send.at[0], y_recv.at[slot], y_dev(distance)
                    )
                    y_sums[slot].start()
    with jax.named_scope("y_sum"):
        for slot in y_sums:
            y_sums[slot].wait_recv()
            own_total = own_total + yr[slot].astype(F32)

    chunk = 128 // owners
    zsrc[...] = own_total.T.astype(BF16)
    owner = z < owners
    quarter = c * 2 + l
    peers = (p1_same, p1_other, core_dev)

    def z_sum(d):
        there = lax.rem(z + d, nz)
        place = pl.ds(pl.multiple_of(there * chunk, 16), chunk)
        return there < owners, remote(zsrc.at[place, :], zr.at[d], zr_send.at[0], zr_recv.at[0], z_dev(d))

    def chunk_of(at):
        return fin.at[pl.ds(pl.multiple_of(quarter * 128 + at * chunk, 16), chunk), :]

    def z_all(d):
        return remote(chunk_of(z), chunk_of(z), za_send.at[0], za_recv.at[d], z_dev(d))

    def hand_on(at):
        for k, device in enumerate(peers):
            remote(chunk_of(at), chunk_of(at), f_send.at[k], f_recv.at[k], device).start()

    with jax.named_scope("z_sum"):
        for d in z_order:
            wanted, copy = z_sum(d)
            pl.when(wanted)(copy.start)

        @pl.when(owner)
        def _():
            piece = zsrc[pl.ds(pl.multiple_of(z * chunk, 16), chunk), :].astype(F32)
            arrived = zr.at[pl.ds(1, nz - 1)]
            remote(arrived, arrived, zr_send.at[0], zr_recv.at[0], z_dev(1)).wait_recv()
            for d in z_order:
                piece = piece + zr[d].astype(F32)
            fin[pl.ds(pl.multiple_of(quarter * 128 + z * chunk, 16), chunk), :] = piece.astype(BF16)
            for d in z_order:
                z_all(d).start()
            hand_on(z)

    with jax.named_scope("z_all"):
        for d in reversed(z_order):
            source = lax.rem(z - d + nz, nz)

            @pl.when(source < owners)
            def _():
                arrived = chunk_of(source)
                remote(arrived, arrived, za_send.at[0], za_recv.at[d], z_dev(d)).wait_recv()
                hand_on(source)

    with jax.named_scope("end_wait"):
        for k, (cc, ll) in enumerate(((c, 1 - l), (1 - c, 1 - l), (1 - c, l))):
            theirs = fin.at[pl.ds(pl.multiple_of((cc * 2 + ll) * 128, 128), 128), :]
            remote(theirs, theirs, f_send.at[k], f_recv.at[k], peers[k]).wait_recv()
    gw_out[...] = fin[...]

    with jax.named_scope("send_waits"):
        own_quarter = fin.at[pl.ds(pl.multiple_of(quarter * 128, 128), 128), :]
        for k, device in enumerate(peers):
            remote(own_quarter, own_quarter, f_send.at[k], f_recv.at[k], device).wait_send()
        for sends, count in ((owner, owners - 1), (jnp.logical_not(owner), owners)):
            if count:
                sent = zr.at[pl.ds(0, count)]
                pl.when(sends)(remote(sent, sent, zr_send.at[0], zr_recv.at[0], z_dev(1)).wait_send)
        sent = zr.at[pl.ds(1, nz - 1)]
        pl.when(owner)(remote(sent, sent, za_send.at[0], za_recv.at[0], z_dev(1)).wait_send)
        for copies in (kv_copies.values(), grad_copies.values()):
            for copy in copies:
                copy.wait_send()
        sent = gs.at[pl.ds(tok, 9 * tok), :]
        remote(sent, sent, g_send.at[0], g_recv.at[1], core_dev).wait_send()
        remote(xs, xs, xs_send.at[0], xs_recv.at[0], core_dev).wait_send()
        sent = ys.at[pl.ds(0, len(y_sums))]
        remote(sent, sent, y_send.at[0], y_recv.at[0], y_dev(1)).wait_send()
        for k, sent in enumerate((from_same, from_other, from_core)):
            remote(sent, sent, xsnd.at[k], xrcv.at[0], core_dev).wait_send()


def write_results(dq_in, gkv_in, gw_in, dq_out, gkv_out, gw_out, wide, sems):
    copies = [
        pltpu.make_async_copy(dq_in, dq_out, sems.at[0]),
        pltpu.make_async_copy(gkv_in, gkv_out, sems.at[1]),
        pltpu.make_async_copy(wide, gw_out, sems.at[2]),
    ]
    copies[0].start()
    copies[1].start()
    wide[...] = gw_in[...].astype(F32)
    copies[2].start()
    for copy in copies:
        copy.wait()


def local(ny, nz, layer_input, query, keys_values, grad_output, logsumexp, delta):
    tok = query.shape[0]
    heads = HQ * tok
    lists = ((3, 0), (6, 7), (4, 1), (5, 2)) if ny == 8 else ((0,), (3,), (2,), (1,))
    size = len(lists[0])
    owners = 8 if nz >= 8 else nz // 2
    dma = pltpu.SemaphoreType.DMA
    any_spec = pl.BlockSpec(memory_space=pl.ANY)
    vmem_spec = pl.BlockSpec(memory_space=pltpu.VMEM)
    results = pl.pallas_call(
        functools.partial(kernel, ny, nz, tok, lists, owners),
        out_shape=(
            pltpu.VMEM((tok, HQ * HD), BF16),
            pltpu.VMEM((tok, 2 * HD), BF16),
            pltpu.VMEM((512, 2 * HD), BF16),
        ),
        in_specs=[any_spec] * 6,
        out_specs=(vmem_spec, vmem_spec, vmem_spec),
        scratch_shapes=[
            pltpu.VMEM((heads, HD), BF16),
            pltpu.VMEM((heads, HD), BF16),
            pltpu.VMEM((HQ, tok), F32),
            pltpu.VMEM((HQ, tok), F32),
            pltpu.VMEM((16, heads), F32),
            pltpu.VMEM((WIN + 2, tok, 2 * HD), BF16),
            pltpu.VMEM(((WIN + 2) * tok, heads), BF16),
            pltpu.VMEM((WIN + 1, tok, 2 * HD), BF16),
            pltpu.VMEM((WIN + 1, tok, 2 * HD), BF16),
            pltpu.VMEM((4, 2 * tok, size * 256), BF16),
            pltpu.VMEM((4, 2 * tok, size * 256), BF16),
            pltpu.VMEM((10 * tok, 2 * HD), BF16),
            pltpu.VMEM((2 * HD, 10 * tok), BF16),
            pltpu.VMEM((3 * size, 256, 128), F32),
            pltpu.VMEM((5 * size, 256, 128), BF16),
            pltpu.VMEM((5 * size, 256, 128), BF16),
            pltpu.VMEM((3 * size, 256, 128), BF16),
            pltpu.VMEM((3 * size, 256, 128), BF16),
            pltpu.VMEM((128, 2 * HD), BF16),
            pltpu.VMEM((nz, 128 // owners, 2 * HD), BF16),
            pltpu.VMEM((512, 2 * HD), BF16),
            dma((5,)),
            dma((1,)),
            dma((WIN + 1,)),
            dma((WIN + 1,)),
            dma((WIN + 1,)),
            dma((WIN + 1,)),
            dma((3,)),
            dma((5,)),
            dma((1,)),
            dma((10,)),
            dma((1,)),
            dma((5 * size,)),
            dma((1,)),
            dma((3 * size,)),
            dma((1,)),
            dma((1,)),
            dma((1,)),
            dma((nz,)),
            dma((3,)),
            dma((3,)),
        ],
        compiler_params=pltpu.CompilerParams(
            collective_id=0, has_side_effects=True, vmem_limit_bytes=56 * 1024 * 1024
        ),
    )(layer_input, query, keys_values, grad_output, logsumexp.T, delta.T)
    return pl.pallas_call(
        write_results,
        out_shape=(
            jax.ShapeDtypeStruct((tok, HQ * HD), BF16),
            jax.ShapeDtypeStruct((tok, 2 * HD), BF16),
            jax.ShapeDtypeStruct((512, 2 * HD), F32),
        ),
        in_specs=[vmem_spec] * 3,
        out_specs=(any_spec, any_spec, any_spec),
        scratch_shapes=[pltpu.VMEM((512, 2 * HD), F32), dma((3,))],
    )(*[pltpu.with_memory_space_constraint(result, pltpu.VMEM) for result in results])


def solution(mesh):
    ny = mesh.shape["outer"] // 2
    nz = mesh.shape["inner"] // 4
    finer = Mesh(mesh.devices.reshape(2, ny, nz, 2, 2), AXES)
    tokens = P(AXES, None)
    return jax.shard_map(
        functools.partial(local, ny, nz),
        mesh=finer,
        in_specs=(tokens,) * 6,
        out_specs=(tokens, tokens, P(("x_hi", "y"), None)),
        check_vma=False,
    )
```

```python
import functools

import jax
import jax.numpy as jnp
from jax import lax
from jax.experimental import pallas as pl
from jax.experimental.pallas import tpu as pltpu
from jax.sharding import Mesh
from jax.sharding import PartitionSpec as P

HD = 128
HQ = 8
WIN = 3
AXES = ("x_hi", "y", "z", "x_lo", "core")
MESH = pl.DeviceIdType.MESH
BF16 = jnp.bfloat16
F32 = jnp.float32
NT = (((1,), (1,)), ((), ()))
LOG2E = 1.4426950408889634


def dot(a, b):
    return jnp.dot(a, b, preferred_element_type=F32)


def dot_nt(a, b):
    return lax.dot_general(a, b, NT, preferred_element_type=F32)


def kernel(
    ny, nz, tok, lists, owners,
    x_hbm, q_hbm, kv_hbm, do_hbm, lse_hbm, delta_hbm,
    dq_out, gkv_out, gw_out,
    qs, dos, lse_in, delta_in, rows, kvb, ds_all, gsend, grecv, x_own, x_pair, gs, gt,
    keep, xs, xr, ys, yr, zsrc, zr, fin,
    load_sem, x_local, kv_send, kv_recv, gr_send, gr_recv, xsnd, xrcv, g_send, g_recv,
    xs_send, xs_recv, y_send, y_recv, zr_send, zr_recv, za_send, za_recv, f_send, f_recv,
):
    h = lax.axis_index("x_hi")
    y = lax.axis_index("y")
    z = lax.axis_index("z")
    l = lax.axis_index("x_lo")
    c = lax.axis_index("core")
    n_inner = nz * 4
    inner = z * 4 + l * 2 + c
    n_outer = 2 * ny
    outer = h * ny + y
    scaling = HD ** (-0.5)

    def inner_dev(step):
        j = lax.rem(inner + step + n_inner, n_inner)
        return {"z": j // 4, "x_lo": lax.rem(j // 2, 2), "core": lax.rem(j, 2)}

    def outer_dev(step):
        j = lax.rem(outer + step + n_outer, n_outer)
        return {"x_hi": j // ny, "y": lax.rem(j, ny)}

    z_m = lax.rem(z + 1 - 2 * l + nz, nz)
    z_n = lax.rem(z - 1 + 2 * l + nz, nz)
    core_dev = {"core": 1 - c}
    p1_same = {"x_lo": 1 - l}
    p1_other = {"x_lo": 1 - l, "core": 1 - c}
    p2_same = {"x_hi": 1 - h, "x_lo": 1 - l}
    p2_other = {"x_hi": 1 - h, "x_lo": 1 - l, "core": 1 - c}
    zm_same, zm_other = {"z": z_m}, {"z": z_m, "core": 1 - c}
    zn_same, zn_other = {"z": z_n}, {"z": z_n, "core": 1 - c}

    def y_dev(d):
        return {"y": lax.rem(y + d, ny)}

    def z_dev(d):
        return {"z": lax.rem(z + d, nz)}

    def remote(src, dst, send, recv, device):
        return pltpu.make_async_remote_copy(
            src_ref=src, dst_ref=dst, send_sem=send, recv_sem=recv, device_id=device, device_id_type=MESH
        )

    z_order = sorted(range(1, nz), key=lambda d: -min(d, nz - d))
    y_order = sorted(range(1, ny), key=lambda d: -min(d, ny - d))

    loads = []
    for k in range(HQ):
        part, cols = pl.ds(k * tok, tok), pl.ds(k * HD, HD)
        pltpu.make_async_copy(q_hbm.at[:, cols], qs.at[part, :], load_sem.at[0]).start()
        pltpu.make_async_copy(do_hbm.at[:, cols], dos.at[part, :], load_sem.at[1]).start()
    loads.append(pltpu.make_async_copy(lse_hbm, lse_in, load_sem.at[2]))
    loads.append(pltpu.make_async_copy(delta_hbm, delta_in, load_sem.at[3]))
    loads.append(pltpu.make_async_copy(kv_hbm, kvb.at[0], load_sem.at[4]))
    for copy in loads:
        copy.start()
    loads.append(pltpu.make_async_copy(qs, qs, load_sem.at[0]))
    loads.append(pltpu.make_async_copy(dos, dos, load_sem.at[1]))

    with jax.named_scope("greet"):
        greeted = [z_dev(d) for d in z_order] + [y_dev(d) for d in y_order] + [outer_dev(1), outer_dev(-1)]
        greeted += [inner_dev(6 * c - 3), inner_dev(2), inner_dev(-2)]
        greeted += [p1_other, p2_other, zm_other, zn_other, p1_same, p2_same, core_dev]
        barrier = pltpu.get_barrier_semaphore()
        for device in greeted:
            pl.semaphore_signal(barrier, inc=1, device_id=device, device_id_type=MESH)
        pl.semaphore_wait(barrier, len(greeted))

    before = (0, 2, 1 + 2 * c, 3 - 2 * c)
    kv_copies = {}
    for slot, device in ((1, inner_dev(2)), (3, inner_dev(1 + 2 * c)), (4, outer_dev(1))):
        kv_copies[slot] = remote(kv_hbm, kvb.at[slot], kv_send.at[slot - 1], kv_recv.at[slot - 1], device)
        kv_copies[slot].start()

    far = 1 - lax.rem(l + z, 2)
    steps_a, steps_b, steps_c, steps_e = lists
    size = len(steps_a)
    distances = [
        list(steps_a),
        list(steps_b),
        [e + far * (s - e) for s, e in zip(steps_c, steps_e)],
        [s + far * (e - s) for s, e in zip(steps_c, steps_e)],
    ]
    def places(which, hh, ll):
        return (
            ((hh, ll), (1 - hh, 1 - ll)),
            ((hh, ll), (hh, 1 - ll)),
            ((hh, ll), (1 - hh, ll)),
            ((hh, 1 - ll), (1 - hh, 1 - ll)),
        )[which]

    shard = 512
    pairs = (
        (0, 0, (h, 1 - l), p1_same, p1_other),
        (1, 1, (1 - h, 1 - l), p2_same, p2_other),
        (2, 3, (h, l), zm_same, zm_other),
        (3, 2, (h, l), zn_same, zn_other),
    )
    with jax.named_scope("issue_columns"):
        for k in range(size):
            for s in range(2):
                slot = pl.ds(k * 256 + s * 128, 128)
                for mine, theirs, (hh, ll), same, other in pairs:
                    shards = lax.rem(y + distances[mine][k], ny) * shard

                    def columns(place, cc):
                        start = place[0] * (ny * shard) + shards + (cc * 2 + place[1]) * 128
                        return x_hbm.at[:, pl.ds(pl.multiple_of(start, 128), 128)]

                    there = places(theirs, hh, ll)[s]
                    here = places(mine, h, l)[s]
                    remote(
                        columns(there, c), x_pair.at[theirs, pl.ds(0, tok), slot],
                        xsnd.at[0], xrcv.at[theirs], same,
                    ).start()
                    remote(
                        columns(there, 1 - c), x_pair.at[theirs, pl.ds(tok, tok), slot],
                        xsnd.at[1], xrcv.at[theirs], other,
                    ).start()
                    remote(
                        columns(here, 1 - c), x_own.at[mine, pl.ds(tok, tok), slot],
                        xsnd.at[2], xrcv.at[4], core_dev,
                    ).start()
                    pltpu.make_async_copy(
                        columns(here, c), x_own.at[mine, pl.ds(0, tok), slot], x_local.at[0]
                    ).start()
    from_own = x_own.at[:, pl.ds(0, tok), :]
    from_core = x_own.at[:, pl.ds(tok, tok), :]
    from_same = x_pair.at[:, pl.ds(0, tok), :]
    from_other = x_pair.at[:, pl.ds(tok, tok), :]

    with jax.named_scope("load_wait"):
        for copy in loads:
            copy.wait()
    for k in range(HQ):
        rows[0:1, k * tok : (k + 1) * tok] = lse_in[k : k + 1, :] * LOG2E
        rows[8:9, k * tok : (k + 1) * tok] = delta_in[k : k + 1, :]

    wide = 2 * tok
    heads = HQ
    key_pos = lax.broadcasted_iota(jnp.int32, (tok, heads * tok), 0)
    lane = lax.broadcasted_iota(jnp.int32, (tok, heads * tok), 1)
    causal = key_pos <= lax.rem(lane, tok)

    def attend(w):
        key = kvb[w, :, :HD]
        value = kvb[w, :, HD:]
        if w == 0:
            penalty = None
        elif w <= WIN:
            penalty = jnp.where(inner >= before[w], 0.0, 1e30).astype(F32)
        else:
            penalty = jnp.where(outer >= 1, 0.0, 1e30).astype(F32)
        grad_key = jnp.zeros((tok, HD), F32)
        grad_value = jnp.zeros((tok, HD), F32)
        for k in range(HQ // heads):
            part = slice(k * heads * tok, (k + 1) * heads * tok)
            query, cotangent = qs[part, :], dos[part, :]
            lse, delta = rows[0:1, part], rows[8:9, part]
            if penalty is not None:
                lse = lse + penalty
            scores = dot_nt(key, query) * (scaling * LOG2E) - lse
            if penalty is None:
                scores = jnp.where(causal, scores, -1e30)
            probs = jnp.exp2(scores)
            grad_probs = dot_nt(value, cotangent)
            grad_scores = (probs * (grad_probs - delta) * scaling).astype(BF16)
            ds_all[w * tok : (w + 1) * tok, part] = grad_scores
            grad_key = grad_key + dot(grad_scores, query)
            grad_value = grad_value + dot(probs.astype(BF16), cotangent)
        return grad_key, grad_value

    with jax.named_scope("own_block"):
        own_key, own_value = attend(0)
    with jax.named_scope("kv_wait"):
        kv_copies[1].wait_recv()
        kv_copies[2] = remote(kvb.at[1], kvb.at[2], kv_send.at[1], kv_recv.at[1], core_dev)
        kv_copies[2].start()
    grad_copies = {}
    for w, device in ((3, inner_dev(2 * c - 3)), (4, outer_dev(-1)), (2, core_dev), (1, inner_dev(-2))):
        if w != 1:
            with jax.named_scope("kv_wait"):
                kv_copies[w].wait_recv()
        with jax.named_scope("attend"):
            grad_key, grad_value = attend(w)
        if w == 1:
            with jax.named_scope("merge_wait"):
                grad_copies[2].wait_recv()
            grad_key = grad_key + grecv[1, :, :HD].astype(F32)
            grad_value = grad_value + grecv[1, :, HD:].astype(F32)
        gsend[w - 1, :, :HD] = grad_key.astype(BF16)
        gsend[w - 1, :, HD:] = grad_value.astype(BF16)
        grad_copies[w] = remote(
            gsend.at[w - 1], grecv.at[w - 1], gr_send.at[w - 1], gr_recv.at[w - 1], device
        )
        grad_copies[w].start()

    with jax.named_scope("grad_query"):
        keys_t = jnp.concatenate([kvb[w, :, :HD] for w in range(WIN + 2)], axis=0).T
        for k in range(HQ // 2):
            part = slice(k * wide, (k + 1) * wide)
            turned = dot(keys_t, ds_all[:, part]).T.astype(BF16)
            dq_out[:, 2 * k * HD : (2 * k + 1) * HD] = turned[:tok]
            dq_out[:, (2 * k + 1) * HD : (2 * k + 2) * HD] = turned[tok:]

    with jax.named_scope("grads_wait"):
        for w in (3, 4, 1):
            grad_copies[w].wait_recv()
            own_key = own_key + grecv[w - 1, :, :HD].astype(F32)
            own_value = own_value + grecv[w - 1, :, HD:].astype(F32)
    grad_kv = jnp.concatenate([own_key, own_value], axis=1).astype(BF16)
    gs[0:tok, :] = grad_kv

    g_copies = {}
    for place, device in ((2, p1_same), (4, p2_same), (8, zm_same), (6, zn_same), (1, core_dev)):
        g_copies[place] = remote(
            gs.at[pl.ds(0, tok), :], gs.at[pl.ds(place * tok, tok), :], g_send.at[0], g_recv.at[place], device
        )
        g_copies[place].start()
    gkv_out[...] = grad_kv

    def turn(pair):
        gt[:, pair * wide : (pair + 1) * wide] = gs[pair * wide : (pair + 1) * wide, :].T

    x_sums = {}

    def push(slot, value, device):
        xs[slot] = value.astype(BF16)
        x_sums[slot] = remote(xs.at[slot], xr.at[slot], xs_send.at[0], xs_recv.at[slot], device)
        x_sums[slot].start()

    with jax.named_scope("core_wait"):
        pltpu.make_async_copy(from_own, from_own, x_local.at[0]).wait()
        remote(from_core, from_core, xsnd.at[2], xrcv.at[4], core_dev).wait_recv()
        g_copies[1].wait_recv()
        turn(0)
    with jax.named_scope("pass_on"):
        for place in (6, 2, 4, 8):
            g_copies[place].wait_recv()
            g_copies[place + 1] = remote(
                gs.at[pl.ds(place * tok, tok), :], gs.at[pl.ds((place + 1) * tok, tok), :],
                g_send.at[0], g_recv.at[place + 1], core_dev,
            )
            g_copies[place + 1].start()

    for mine in (2, 0, 1, 3):
        with jax.named_scope("pair_wait"):
            place = {0: 2, 1: 4, 2: 6, 3: 8}[mine]
            g_copies[place + 1].wait_recv()
            turn(place // 2)
            remote(x_pair.at[mine], x_pair.at[mine], xsnd.at[0], xrcv.at[mine], pairs[mine][3]).wait_recv()
        with jax.named_scope("multiply"):
            for k in range(size):
                cols = slice(k * 256, (k + 1) * 256)
                product = dot(gt[:, :wide], x_own[mine, :, cols])
                product = product + dot(gt[:, place * tok : (place + 2) * tok], x_pair[mine, :, cols])
                first, second = product[:, :128], product[:, 128:]
                if mine == 3:
                    through = 2 * size + k
                    x_sums[through].wait_recv()
                    if k % 2 == 0:
                        second = second + xr[through].astype(F32)
                    else:
                        first = first + xr[through].astype(F32)
                    push(3 * size + k, first, p1_same)
                    push(4 * size + k, second, p2_same)
                else:
                    keep[mine * size + k] = first
                    push(mine * size + k, second, (p2_same, p1_same, p2_same if k % 2 else p1_same)[mine])

    y_sums = {}
    own_total = None
    with jax.named_scope("x_sum"):
        for mine in (0, 1, 2):
            for k in range(size):
                slot = mine * size + k
                total = keep[slot]
                for source in (3 * size + k, 4 * size + k) if mine == 2 else (slot,):
                    x_sums[source].wait_recv()
                    total = total + xr[source].astype(F32)
                distance = distances[mine][k]
                if mine < 2 and distance == 0:
                    own_total = total
                else:
                    ys[slot] = total.astype(BF16)
                    y_sums[slot] = remote(
                        ys.at[slot], yr.at[slot], y_send.at[0], y_recv.at[slot], y_dev(distance)
                    )
                    y_sums[slot].start()
    with jax.named_scope("y_sum"):
        for slot in y_sums:
            y_sums[slot].wait_recv()
            own_total = own_total + yr[slot].astype(F32)

    chunk = 128 // owners
    zsrc[...] = own_total.T.astype(BF16)
    owner = z < owners
    quarter = c * 2 + l
    peers = (p1_same, p1_other, core_dev)

    def z_sum(d):
        there = lax.rem(z + d, nz)
        place = pl.ds(pl.multiple_of(there * chunk, 16), chunk)
        return there < owners, remote(zsrc.at[place, :], zr.at[d], zr_send.at[0], zr_recv.at[0], z_dev(d))

    def chunk_of(at):
        return fin.at[pl.ds(pl.multiple_of(quarter * 128 + at * chunk, 16), chunk), :]

    def z_all(d):
        return remote(chunk_of(z), chunk_of(z), za_send.at[0], za_recv.at[d], z_dev(d))

    def hand_on(at):
        for k, device in enumerate(peers):
            remote(chunk_of(at), chunk_of(at), f_send.at[k], f_recv.at[k], device).start()

    with jax.named_scope("z_sum"):
        for d in z_order:
            wanted, copy = z_sum(d)
            pl.when(wanted)(copy.start)

        @pl.when(owner)
        def _():
            piece = zsrc[pl.ds(pl.multiple_of(z * chunk, 16), chunk), :].astype(F32)
            arrived = zr.at[pl.ds(1, nz - 1)]
            remote(arrived, arrived, zr_send.at[0], zr_recv.at[0], z_dev(1)).wait_recv()
            for d in z_order:
                piece = piece + zr[d].astype(F32)
            fin[pl.ds(pl.multiple_of(quarter * 128 + z * chunk, 16), chunk), :] = piece.astype(BF16)
            for d in z_order:
                z_all(d).start()
            hand_on(z)

    with jax.named_scope("z_all"):
        for d in reversed(z_order):
            source = lax.rem(z - d + nz, nz)

            @pl.when(source < owners)
            def _():
                arrived = chunk_of(source)
                remote(arrived, arrived, za_send.at[0], za_recv.at[d], z_dev(d)).wait_recv()
                hand_on(source)

    with jax.named_scope("end_wait"):
        for k, (cc, ll) in enumerate(((c, 1 - l), (1 - c, 1 - l), (1 - c, l))):
            theirs = fin.at[pl.ds(pl.multiple_of((cc * 2 + ll) * 128, 128), 128), :]
            remote(theirs, theirs, f_send.at[k], f_recv.at[k], peers[k]).wait_recv()
    gw_out[...] = fin[...]

    with jax.named_scope("send_waits"):
        own_quarter = fin.at[pl.ds(pl.multiple_of(quarter * 128, 128), 128), :]
        for k, device in enumerate(peers):
            remote(own_quarter, own_quarter, f_send.at[k], f_recv.at[k], device).wait_send()
        for sends, count in ((owner, owners - 1), (jnp.logical_not(owner), owners)):
            if count:
                sent = zr.at[pl.ds(0, count)]
                pl.when(sends)(remote(sent, sent, zr_send.at[0], zr_recv.at[0], z_dev(1)).wait_send)
        sent = zr.at[pl.ds(1, nz - 1)]
        pl.when(owner)(remote(sent, sent, za_send.at[0], za_recv.at[0], z_dev(1)).wait_send)
        for copies in (kv_copies.values(), grad_copies.values()):
            for copy in copies:
                copy.wait_send()
        sent = gs.at[pl.ds(tok, 9 * tok), :]
        remote(sent, sent, g_send.at[0], g_recv.at[1], core_dev).wait_send()
        remote(xs, xs, xs_send.at[0], xs_recv.at[0], core_dev).wait_send()
        sent = ys.at[pl.ds(0, len(y_sums))]
        remote(sent, sent, y_send.at[0], y_recv.at[0], y_dev(1)).wait_send()
        for k, sent in enumerate((from_same, from_other, from_core)):
            remote(sent, sent, xsnd.at[k], xrcv.at[0], core_dev).wait_send()


def write_results(dq_in, gkv_in, gw_in, dq_out, gkv_out, gw_out, wide, sems):
    copies = [
        pltpu.make_async_copy(dq_in, dq_out, sems.at[0]),
        pltpu.make_async_copy(gkv_in, gkv_out, sems.at[1]),
        pltpu.make_async_copy(wide, gw_out, sems.at[2]),
    ]
    copies[0].start()
    copies[1].start()
    wide[...] = gw_in[...].astype(F32)
    copies[2].start()
    for copy in copies:
        copy.wait()


def local(ny, nz, layer_input, query, keys_values, grad_output, logsumexp, delta):
    tok = query.shape[0]
    heads = HQ * tok
    lists = ((6, 0), (7, 1), (4, 2), (3, 5)) if ny == 8 else ((0,), (3,), (2,), (1,))
    size = len(lists[0])
    owners = 8 if nz >= 8 else nz // 2
    dma = pltpu.SemaphoreType.DMA
    any_spec = pl.BlockSpec(memory_space=pl.ANY)
    vmem_spec = pl.BlockSpec(memory_space=pltpu.VMEM)
    results = pl.pallas_call(
        functools.partial(kernel, ny, nz, tok, lists, owners),
        out_shape=(
            pltpu.VMEM((tok, HQ * HD), BF16),
            pltpu.VMEM((tok, 2 * HD), BF16),
            pltpu.VMEM((512, 2 * HD), BF16),
        ),
        in_specs=[any_spec] * 6,
        out_specs=(vmem_spec, vmem_spec, vmem_spec),
        scratch_shapes=[
            pltpu.VMEM((heads, HD), BF16),
            pltpu.VMEM((heads, HD), BF16),
            pltpu.VMEM((HQ, tok), F32),
            pltpu.VMEM((HQ, tok), F32),
            pltpu.VMEM((16, heads), F32),
            pltpu.VMEM((WIN + 2, tok, 2 * HD), BF16),
            pltpu.VMEM(((WIN + 2) * tok, heads), BF16),
            pltpu.VMEM((WIN + 1, tok, 2 * HD), BF16),
            pltpu.VMEM((WIN + 1, tok, 2 * HD), BF16),
            pltpu.VMEM((4, 2 * tok, size * 256), BF16),
            pltpu.VMEM((4, 2 * tok, size * 256), BF16),
            pltpu.VMEM((10 * tok, 2 * HD), BF16),
            pltpu.VMEM((2 * HD, 10 * tok), BF16),
            pltpu.VMEM((3 * size, 256, 128), F32),
            pltpu.VMEM((5 * size, 256, 128), BF16),
            pltpu.VMEM((5 * size, 256, 128), BF16),
            pltpu.VMEM((3 * size, 256, 128), BF16),
            pltpu.VMEM((3 * size, 256, 128), BF16),
            pltpu.VMEM((128, 2 * HD), BF16),
            pltpu.VMEM((nz, 128 // owners, 2 * HD), BF16),
            pltpu.VMEM((512, 2 * HD), BF16),
            dma((5,)),
            dma((1,)),
            dma((WIN + 1,)),
            dma((WIN + 1,)),
            dma((WIN + 1,)),
            dma((WIN + 1,)),
            dma((3,)),
            dma((5,)),
            dma((1,)),
            dma((10,)),
            dma((1,)),
            dma((5 * size,)),
            dma((1,)),
            dma((3 * size,)),
            dma((1,)),
            dma((1,)),
            dma((1,)),
            dma((nz,)),
            dma((3,)),
            dma((3,)),
        ],
        compiler_params=pltpu.CompilerParams(
            collective_id=0, has_side_effects=True, vmem_limit_bytes=56 * 1024 * 1024
        ),
    )(layer_input, query, keys_values, grad_output, logsumexp.T, delta.T)
    return pl.pallas_call(
        write_results,
        out_shape=(
            jax.ShapeDtypeStruct((tok, HQ * HD), BF16),
            jax.ShapeDtypeStruct((tok, 2 * HD), BF16),
            jax.ShapeDtypeStruct((512, 2 * HD), F32),
        ),
        in_specs=[vmem_spec] * 3,
        out_specs=(any_spec, any_spec, any_spec),
        scratch_shapes=[pltpu.VMEM((512, 2 * HD), F32), dma((3,))],
    )(*[pltpu.with_memory_space_constraint(result, pltpu.VMEM) for result in results])


def solution(mesh):
    ny = mesh.shape["outer"] // 2
    nz = mesh.shape["inner"] // 4
    finer = Mesh(mesh.devices.reshape(2, ny, nz, 2, 2), AXES)
    tokens = P(AXES, None)
    return jax.shard_map(
        functools.partial(local, ny, nz),
        mesh=finer,
        in_specs=(tokens,) * 6,
        out_specs=(tokens, tokens, P(("x_hi", "y"), None)),
        check_vma=False,
    )
```
